256 devices in a mesh: dp: 4 (over x), seq: 32 (over y, z_lo, core), head: 2 (over z_hi).
Axes of the slice: x: 4, y: 4, z: 8 (z_hi: 2, z_lo: 4; z = z_hi * 4 + z_lo), core: 2. Of those that a mesh axis runs over, the one named last changes fastest.
Arguments:
- byte_states: bfloat16 [4, 8192, 2048], P('dp', 'seq', 'head'), may hold values from -6 to 6
- segment_ids: int32 [4, 64, 128], P('dp', 'seq'), may hold values from 0 to 15, never falling along the last dimension, each value on 1 to 32 neighbouring positions
- w_query: bfloat16 [2048, 1024], P(None, 'head'), may hold values from -1 to 1
- w_key: bfloat16 [2048, 1024], P(None, 'head'), may hold values from -1 to 1
- w_value: bfloat16 [2048, 1024], P(None, 'head'), may hold values from -0.125 to 0.125
- d_out: bfloat16 [4, 1024, 1024], P('dp', 'seq', 'head'), may hold values from -6 to 6
Outputs:
- d_bytes: bfloat16 [4, 8192, 2048], P('dp', 'seq', 'head')
- grad_query: float32 [2048, 1024], P(('dp', 'seq'), 'head')
- grad_key: float32 [2048, 1024], P(('dp', 'seq'), 'head')
- grad_value: float32 [2048, 1024], P(('dp', 'seq'), 'head')
The draws below stay inside these ranges and needn't reach their ends.
Inputs may be any that keep to these rules, and one draw needn't show every extreme that they name: `segment_ids`: in each block of 128 bytes the slots never fall, every one of the 16 slots holds 1 to 32 bytes, and one holds exactly 32.
All inputs are finite; a program needn't handle non-finite values.
Results may differ from the reference program's by a relative error of at most 0.04.
Values may be sent and summed in bfloat16 or wider, within the bound.
No kernel may reach another device: no remote copies, remote signals or barrier semaphores. Data moves between devices by JAX's collectives and lax.ppermute only.
A program may use at most 64 MiB of HBM per device.

```python
import math
import jax
import jax.numpy as jnp
import numpy as np
from jax import lax

D = 2048
HEADS = 8
HEAD_DIM = 128
BLOCK_BYTES = 128
SLOTS = 16
SEQ_BYTES = 8192
BLOCKS = 64
SHORT = 1024
HD = 1024
N_DP = 4


def draw_byte_states(key, part):
    key = jax.random.fold_in(key, 11)
    noise_key = jax.random.fold_in(key, 0)
    states = jax.random.truncated_normal(noise_key, -6.0, 6.0, (N_DP, SEQ_BYTES, D), jnp.float32)
    return states.astype(jnp.bfloat16)


def draw_w_query(key, part):
    key = jax.random.fold_in(key, 21)
    base = jax.random.truncated_normal(key, -3.0, 3.0, (D, HD), jnp.float32) / math.sqrt(D)
    return base.astype(jnp.bfloat16)


def draw_w_key(key, part):
    key = jax.random.fold_in(key, 31)
    base = jax.random.truncated_normal(key, -3.0, 3.0, (D, HD), jnp.float32) / math.sqrt(D)
    return base.astype(jnp.bfloat16)


def levels(key, extent, cuts, smallest, high):
    level, own = 1.0, jax.random.fold_in(key, 6)
    for position, blocks in cuts:
        draws = jnp.exp(jax.random.uniform(jax.random.fold_in(own, position), (blocks,), jnp.float32, smallest / len(cuts), high / len(cuts)))
        level = level * jnp.repeat(draws, extent[position] // blocks).reshape([-1 if axis == position else 1 for axis in range(len(extent))])
    return level


def length_profile(amount, total, limit, skew):
    weights = [(1 << 20) // math.isqrt(rank ** skew) + 1 for rank in range(2, amount + 1)]
    spare, given = total - limit - (amount - 1), [1] * (amount - 1)
    while spare > 0:
        candidates = [i for i in range(amount - 1) if given[i] < limit]
        pool, left = sum([weights[i] for i in candidates]), spare
        for i in candidates:
            addition = min(limit - given[i], max(1, left * weights[i] // pool), spare)
            given[i] = given[i] + addition
            spare = spare - addition
    return np.array([limit] + given)


def ragged(own_key, amount, total, bound, lean):
    if amount == 2:
        one = jax.random.randint(own_key, (), max(1, total - bound), min(bound, total - 1) + 1)
        return jnp.stack([one, total - one])
    lengths = jnp.asarray(length_profile(amount, total, bound, lean), jnp.int32)
    twos = (amount - 1) // 2
    giver, receiver = lengths[1:1 + 2 * twos:2], lengths[2:2 + 2 * twos:2]
    margin = jnp.minimum(giver - 1, bound - receiver)
    shifted = jax.random.randint(jax.random.fold_in(own_key, 1), (twos,), 0, 1 << 20) % (margin + 1)
    lengths = lengths.at[1:1 + 2 * twos:2].set(giver - shifted).at[2:2 + 2 * twos:2].set(receiver + shifted)
    return lengths[jax.random.permutation(jax.random.fold_in(own_key, 2), amount)]


def gaussian(rng, dims, deviation, limit, shards=(), kind=jnp.bfloat16):
    entries = jax.random.normal(rng, dims, jnp.float32) * deviation
    if len(shards) > 0:
        entries = levels(rng, dims, shards, -0.22, 0.18) * entries
    return jnp.clip(entries, min=-limit, max=limit).astype(kind)


def setup_inputs(seed: int = 0) -> dict:
    arg_keys = jax.random.split(jax.random.key(seed), 7)
    return {
        "byte_states": draw_byte_states(jax.random.fold_in(arg_keys[6], 71), 0),
        "segment_ids": jax.vmap(lambda own: jnp.searchsorted(jnp.cumsum(ragged(own, SLOTS, BLOCK_BYTES, 32, 2)), jnp.arange(BLOCK_BYTES), side="right"))(jax.random.split(arg_keys[1], N_DP * BLOCKS)).reshape((N_DP, BLOCKS, BLOCK_BYTES)).astype(jnp.int32),
        "w_query": draw_w_query(jax.random.fold_in(arg_keys[6], 71), 0),
        "w_key": draw_w_key(jax.random.fold_in(arg_keys[6], 71), 0),
        "w_value": gaussian(arg_keys[4], (D, HD), D ** -0.5, 0.125, ((1, 2),)),
        "d_out": gaussian(arg_keys[5], (N_DP, SHORT, HD), 1.0, 6.0, ((0, 4), (1, 32), (2, 2))),
    }


NEG = -1e+30

def head_backward(parts):
    query_h, key_h, value_h, grad_h = parts
    length = query_h.shape[0]
    softmax_scale = 1.0 / math.sqrt(HEAD_DIM)
    positions = jnp.arange(length, dtype=jnp.int32)
    raw = jnp.dot(query_h, key_h.T, preferred_element_type=jnp.float32) * softmax_scale
    scores = jnp.where(positions[None, :] <= positions[:, None], raw, NEG)
    row_max = lax.optimization_barrier(jnp.max(scores, axis=1, keepdims=True))
    expd = jnp.exp(scores - row_max)
    attn_probs = expd / lax.optimization_barrier(jnp.sum(expd, axis=1, keepdims=True))
    d_prob = jnp.dot(grad_h, value_h.T, preferred_element_type=jnp.float32)
    delta = lax.optimization_barrier(jnp.sum(attn_probs * d_prob, axis=1, keepdims=True))
    d_score = (attn_probs * (d_prob - delta)).astype(jnp.bfloat16)
    probs_low = attn_probs.astype(jnp.bfloat16)
    d_query = (jnp.dot(d_score, key_h, preferred_element_type=jnp.float32) * softmax_scale).astype(jnp.bfloat16)
    d_key = (jnp.dot(d_score.T, query_h, preferred_element_type=jnp.float32) * softmax_scale).astype(jnp.bfloat16)
    d_value = jnp.dot(probs_low.T, grad_h, preferred_element_type=jnp.float32).astype(jnp.bfloat16)
    return (d_query, d_key, d_value)

def split_heads(matrix):
    return jnp.moveaxis(matrix.reshape(matrix.shape[0], HEADS, HEAD_DIM), 1, 0)

def join_heads(stacked):
    return jnp.moveaxis(stacked, 0, 1).reshape(stacked.shape[1], HEADS * HEAD_DIM)

def one_sequence(byte_rows, slot_ids, grad_rows, w_query, w_key, w_value):
    blocks = slot_ids.shape[0]
    slot_range = jnp.arange(SLOTS, dtype=jnp.int32)
    onehot = (slot_ids[:, None, :] == slot_range[None, :, None]).astype(jnp.float32)
    counts = lax.optimization_barrier(jnp.sum(onehot, axis=2)).reshape(-1, 1)
    states = byte_rows.reshape(blocks, BLOCK_BYTES, D).astype(jnp.float32)
    sums = jnp.einsum('kjt,ktd->kjd', onehot, states, precision=lax.Precision.HIGHEST).reshape(-1, D)
    pooled = (sums / counts).astype(jnp.bfloat16)
    query = jnp.dot(pooled, w_query, preferred_element_type=jnp.float32).astype(jnp.bfloat16)
    key = jnp.dot(pooled, w_key, preferred_element_type=jnp.float32).astype(jnp.bfloat16)
    value = jnp.dot(pooled, w_value, preferred_element_type=jnp.float32).astype(jnp.bfloat16)
    d_query, d_key, d_value = lax.map(head_backward, (split_heads(query), split_heads(key), split_heads(value), split_heads(grad_rows)))
    d_query = join_heads(d_query)
    d_key = join_heads(d_key)
    d_value = join_heads(d_value)
    pooled_t = pooled.T
    grad_q = jnp.dot(pooled_t, d_query, preferred_element_type=jnp.float32)
    grad_k = jnp.dot(pooled_t, d_key, preferred_element_type=jnp.float32)
    grad_v = jnp.dot(pooled_t, d_value, preferred_element_type=jnp.float32)
    d_pooled = jnp.dot(d_query, w_query.T, preferred_element_type=jnp.float32)
    d_pooled = d_pooled + jnp.dot(d_key, w_key.T, preferred_element_type=jnp.float32)
    d_pooled = d_pooled + jnp.dot(d_value, w_value.T, preferred_element_type=jnp.float32)
    per_slot = d_pooled / counts
    block_index = jnp.arange(blocks, dtype=jnp.int32)[:, None] * SLOTS
    slot_index = (block_index + slot_ids.astype(jnp.int32)).reshape(-1)
    d_rows = jnp.take(per_slot, slot_index, axis=0).astype(jnp.bfloat16)
    return (d_rows, grad_q, grad_k, grad_v)

def reference(byte_states, segment_ids, w_query, w_key, w_value, d_out):
    outputs = []
    grad_query = jnp.zeros((D, HEADS * HEAD_DIM), jnp.float32)
    grad_key = jnp.zeros((D, HEADS * HEAD_DIM), jnp.float32)
    grad_value = jnp.zeros((D, HEADS * HEAD_DIM), jnp.float32)
    for replica in range(N_DP):
        d_rows, grad_q, grad_k, grad_v = one_sequence(byte_states[replica], segment_ids[replica], d_out[replica], w_query, w_key, w_value)
        outputs.append(d_rows)
        grad_query = grad_query + grad_q
        grad_key = grad_key + grad_k
        grad_value = grad_value + grad_v
    return (jnp.stack(outputs), grad_query, grad_key, grad_value)
```

```python
import functools
import math

import jax
import jax.numpy as jnp
import numpy as np
from jax import lax
from jax.experimental import pallas as pl
from jax.experimental.pallas import tpu as pltpu
from jax.sharding import Mesh, PartitionSpec as P

HEAD_DIM = 128
BLOCK_BYTES = 128
SLOTS = 16
SCALE = 1.0 / math.sqrt(HEAD_DIM)
NEG = -1e30
F32 = jnp.float32
BF16 = jnp.bfloat16

VMEM = pl.BlockSpec(memory_space=pltpu.VMEM)
SMEM = pl.BlockSpec(memory_space=pltpu.SMEM)


def project_kernel(place_ref, pooled_ref, grad_ref, wq_ref, wk_ref, wv_ref, out_ref, chunk_ref):
    rows = jnp.concatenate(
        [pooled_ref[:, half].reshape(128, 1024) for half in range(2)], axis=1
    )
    for part, w_ref in enumerate((wq_ref, wk_ref, wv_ref)):
        made = jnp.dot(rows, w_ref[...], preferred_element_type=F32).astype(BF16)
        for head in range(4):
            out_ref[head, :, part * 128 : (part + 1) * 128] = made[:, head * 128 : (head + 1) * 128]
    for head in range(4):
        out_ref[head, :, 384:512] = grad_ref[:, head * 128 : (head + 1) * 128]
    zl = place_ref[0]
    group = lax.broadcasted_iota(jnp.int32, (128, 128), 1) // 16
    tiles = [jnp.zeros((128, 128), F32) for _ in range(4)]
    for block in range(16):
        piece = rows[:, block * 128 : (block + 1) * 128].astype(F32)
        for core in range(2):
            shift = lax.rem((block % 8) * 16 - core * 16 - zl * 32 + 256, 128)
            moved = pltpu.roll(piece, shift, 1)
            tile = core * 2 + block // 8
            tiles[tile] = jnp.where(group == block % 8, moved, tiles[tile])
    for tile in range(4):
        chunk_ref[:, tile * 128 : (tile + 1) * 128] = tiles[tile].astype(BF16)


def attention_kernel(place_ref, own_ref, peer_ref, d_ref, all_ref, dk_ref, dv_ref):
    core = place_ref[1]
    for y in range(4):
        for zl in range(4):
            all_ref[y, zl, core] = own_ref[y, zl]
            all_ref[y, zl, 1 - core] = peer_ref[y, zl]
    dk_ref[...] = jnp.zeros_like(dk_ref)
    dv_ref[...] = jnp.zeros_like(dv_ref)
    nt = (((1,), (1,)), ((), ()))
    tn = (((0,), (0,)), ((), ()))

    def put(y, part, value):
        value = value.reshape(4, 2, 32, 128)
        for zl in range(4):
            for c in range(2):
                other = jnp.where(core == c, 0, 1)
                d_ref[other, y, zl, :, part * 128 : (part + 1) * 128] = value[zl, c]

    def rows_of(y):
        return all_ref[y].reshape(256, 512)

    for i in range(4):
        mine = rows_of(i)
        width = (i + 1) * 256
        keys = jnp.concatenate([rows_of(y)[:, 128:256] for y in range(i + 1)], axis=0)
        values = jnp.concatenate([rows_of(y)[:, 256:384] for y in range(i + 1)], axis=0)
        query, grad = mine[:, 0:128], mine[:, 384:512]
        scores = lax.dot_general(query, keys, nt, preferred_element_type=F32) * SCALE
        q_pos = i * 256 + lax.broadcasted_iota(jnp.int32, (256, width), 0)
        k_pos = lax.broadcasted_iota(jnp.int32, (256, width), 1)
        scores = jnp.where(k_pos <= q_pos, scores, NEG)
        expd = jnp.exp(scores - jnp.max(scores, axis=1, keepdims=True))
        probs = expd * (1.0 / jnp.sum(expd, axis=1, keepdims=True))
        d_prob = lax.dot_general(grad, values, nt, preferred_element_type=F32)
        delta = jnp.sum(probs * d_prob, axis=1, keepdims=True)
        d_score = (probs * (d_prob - delta)).astype(BF16)
        low = probs.astype(BF16)
        put(i, 0, (jnp.dot(d_score, keys, preferred_element_type=F32) * SCALE).astype(BF16))
        dk_ref[0:width, :] += lax.dot_general(d_score, query, tn, preferred_element_type=F32)
        dv_ref[0:width, :] += lax.dot_general(low, grad, tn, preferred_element_type=F32)
    for i in range(4):
        put(i, 1, (dk_ref[i * 256 : (i + 1) * 256, :] * SCALE).astype(BF16))
        put(i, 2, dv_ref[i * 256 : (i + 1) * 256, :].astype(BF16))


def params(mib):
    return pltpu.CompilerParams(vmem_limit_bytes=mib << 20)


def swap(x, axis):
    return lax.ppermute(x, axis, [(0, 1), (1, 0)])


def body(byte_states, segment_ids, w_query, w_key, w_value, d_out):
    zl, core, zh = (lax.axis_index(a) for a in ("zl", "core", "zh"))
    place = jnp.stack([zl, core, zh]).astype(jnp.int32)
    slot_ids = segment_ids[0]
    blocks = slot_ids.shape[0]
    slot_range = jnp.arange(SLOTS, dtype=jnp.int32)
    onehot = slot_ids[:, None, :] == slot_range[None, :, None]
    counts = jnp.sum(onehot.astype(F32), axis=2)
    local_bytes = byte_states[0].reshape(blocks, BLOCK_BYTES, byte_states.shape[2])
    sums = jnp.einsum(
        "kjt,ktd->kjd", onehot.astype(BF16), local_bytes, preferred_element_type=F32
    )
    pooled_half = (sums / counts[:, :, None]).reshape(blocks * SLOTS, -1).astype(BF16)

    with jax.named_scope("gather_line_rows"):
        grad_line = lax.all_gather(d_out[0], "zl", axis=0, tiled=True)
        pooled_line = lax.all_to_all(
            jnp.broadcast_to(pooled_half[None], (8, 32, 1024)), ("zl", "zh"), 0, 0, tiled=True
        ).reshape(4, 2, 32, 1024)

    with jax.named_scope("project"):
        packed, chunk = pl.pallas_call(
            project_kernel,
            out_shape=(
                jax.ShapeDtypeStruct((4, 128, 512), BF16),
                jax.ShapeDtypeStruct((128, 512), BF16),
            ),
            in_specs=[SMEM] + [VMEM] * 5,
            out_specs=(VMEM, VMEM),
            compiler_params=params(40),
        )(place, pooled_line, grad_line, w_query, w_key, w_value)

    with jax.named_scope("share_chunk"):
        chunk_rows = lax.all_gather(chunk, "y", axis=0, tiled=True)
        low, high = chunk_rows[:, :256], chunk_rows[:, 256:]
        chunk_own = jnp.where(core == 0, low, high)
        chunk_peer = swap(jnp.where(core == 0, high, low), "core")

    with jax.named_scope("share_heads"):
        own = lax.all_to_all(packed, "y", 0, 0, tiled=True).reshape(4, 4, 32, 512)
        peer = swap(own, "core")

    with jax.named_scope("attention"):
        d_rows = pl.pallas_call(
            attention_kernel,
            out_shape=jax.ShapeDtypeStruct((2, 4, 4, 32, 384), BF16),
            in_specs=[SMEM, VMEM, VMEM],
            out_specs=VMEM,
            scratch_shapes=[
                pltpu.VMEM((4, 4, 2, 32, 512), BF16),
                pltpu.VMEM((1024, 128), F32),
                pltpu.VMEM((1024, 128), F32),
            ],
            compiler_params=params(40),
        )(place, own, peer)

    with jax.named_scope("return_rows"):
        back = lax.dynamic_index_in_dim(d_rows[0], zl, axis=1, keepdims=False)
        back = lax.all_to_all(back, "y", 0, 0, tiled=True)

    tn = (((0,), (0,)), ((), ()))
    with jax.named_scope("weight_grads"):
        partial = lax.dot_general(
            chunk_own, d_rows[0].reshape(512, 384), tn, preferred_element_type=F32
        ) + lax.dot_general(
            chunk_peer, d_rows[1].reshape(512, 384), tn, preferred_element_type=F32
        )
        parts = lax.all_to_all(
            partial.astype(BF16).reshape(16, 16, 384), ("dp", "y"), 0, 0, tiled=True
        ).reshape(4, 4, 16, 384)
        summed = jnp.sum(parts.astype(F32), axis=0)
        grads = [
            jnp.transpose(summed[:, :, p * 128 : (p + 1) * 128], (1, 0, 2)).reshape(16, 512)
            for p in range(3)
        ]

    with jax.named_scope("back_project"):
        d_pooled = 0.0
        for p, w in enumerate((w_query, w_key, w_value)):
            rows = jnp.transpose(back[:, :, p * 128 : (p + 1) * 128], (1, 0, 2)).reshape(32, 512)
            d_pooled = d_pooled + lax.dot_general(
                rows, w, (((1,), (1,)), ((), ())), preferred_element_type=F32
            )
        left, right = d_pooled[:, :1024], d_pooled[:, 1024:]
        keep = jnp.where(zh == 0, left, right)
        send = jnp.where(zh == 0, right, left).astype(BF16)
        total = keep + swap(send, "zh").astype(F32)
        per_slot = (total / counts.reshape(-1, 1)).astype(BF16).reshape(blocks, SLOTS, 1024)
        d_bytes = jnp.einsum(
            "kjt,kjd->ktd", onehot.astype(BF16), per_slot, preferred_element_type=F32
        )
        d_bytes = d_bytes.astype(BF16).reshape(1, blocks * BLOCK_BYTES, 1024)
    return (d_bytes, *grads)


def solution(mesh):
    fine = Mesh(
        np.asarray(mesh.devices).reshape(4, 4, 4, 2, 2), ("dp", "y", "zl", "core", "zh")
    )
    seq = ("y", "zl", "core")
    return jax.shard_map(
        body,
        mesh=fine,
        in_specs=(
            P("dp", seq, "zh"),
            P("dp", seq, None),
            P(None, "zh"),
            P(None, "zh"),
            P(None, "zh"),
            P("dp", seq, "zh"),
        ),
        out_specs=(
            P("dp", seq, "zh"),
            P(("dp", *seq), "zh"),
            P(("dp", *seq), "zh"),
            P(("dp", *seq), "zh"),
        ),
        check_vma=False,
    )
```

```python
import math

import jax
import jax.numpy as jnp
import numpy as np
from jax import lax
from jax.experimental import pallas as pl
from jax.experimental.pallas import tpu as pltpu
from jax.sharding import Mesh, PartitionSpec as P

HEAD_DIM = 128
SLOTS = 16
SCALE = 1.0 / math.sqrt(HEAD_DIM)
NEG = -1e30
F32 = jnp.float32
BF16 = jnp.bfloat16
NT = (((1,), (1,)), ((), ()))
TN = (((0,), (0,)), ((), ()))

VMEM = pl.BlockSpec(memory_space=pltpu.VMEM)


def slots_of(ids_ref, block):
    slot = lax.broadcasted_iota(jnp.int32, (SLOTS, 128), 0)
    return (ids_ref[block : block + 1, :] == slot).astype(F32)


def pool_kernel(ids_hbm, bytes_hbm, pooled_ref, ids_ref, bytes_ref, sems):
    copies = [
        pltpu.make_async_copy(ids_hbm, ids_ref, sems.at[0]),
        pltpu.make_async_copy(bytes_hbm, bytes_ref, sems.at[1]),
    ]
    for copy in copies:
        copy.start()
    for copy in copies:
        copy.wait()
    for block in range(2):
        onehot = slots_of(ids_ref, block)
        sums = jnp.dot(
            onehot.astype(BF16),
            bytes_ref[block * 128 : (block + 1) * 128, :],
            preferred_element_type=F32,
        )
        mean = (sums / jnp.sum(onehot, axis=1, keepdims=True)).astype(BF16)
        for device in range(8):
            pooled_ref[device, block * SLOTS : (block + 1) * SLOTS, :] = mean


def project_kernel(
    pooled_ref, grad0_ref, grad1_ref, grad2_ref, grad3_ref, wq_ref, wk_ref, wv_ref,
    out0_ref, out1_ref, out2_ref, out3_ref, chunk_ref, heads_ref,
):
    y, zl = lax.axis_index("y"), lax.axis_index("zl")
    halves = [pooled_ref[:, half].reshape(128, 1024) for half in range(2)]
    group = lax.broadcasted_iota(jnp.int32, (128, 128), 1) // 16
    tiles = [jnp.zeros((128, 128), F32) for _ in range(4)]
    for block in range(16):
        first = (block % 8) * 128
        piece = halves[block // 8][:, first : first + 128].astype(F32)
        for core in range(2):
            shift = lax.rem((block % 8) * 16 - core * 16 - zl * 32 + 256, 128)
            moved = pltpu.roll(piece, shift, 1)
            tile = core * 2 + block // 8
            tiles[tile] = jnp.where(group == block % 8, moved, tiles[tile])
    for tile in range(4):
        chunk_ref[:, tile * 128 : (tile + 1) * 128] = tiles[tile].astype(BF16)
    for step, grad_ref in enumerate((grad0_ref, grad1_ref, grad2_ref, grad3_ref)):
        source = lax.rem(zl - step + 4, 4)
        for head in range(4):
            heads_ref[head, source, :, 384:512] = grad_ref[:, head * 128 : (head + 1) * 128]
    rows = jnp.concatenate(halves, axis=1)
    for part, w_ref in enumerate((wq_ref, wk_ref, wv_ref)):
        made = jnp.dot(rows, w_ref[...], preferred_element_type=F32)
        made = made.astype(BF16).reshape(4, 32, 512)
        for head in range(4):
            lanes = slice(head * 128, (head + 1) * 128)
            heads_ref[head, :, :, part * 128 : (part + 1) * 128] = made[:, :, lanes]
    for step, out_ref in enumerate((out0_ref, out1_ref, out2_ref, out3_ref)):
        out_ref[...] = heads_ref[lax.rem(y + step, 4)]


def attention_kernel(*refs):
    own_refs, peer_refs = refs[0:4], refs[4:8]
    d_ref, back_refs, (all_ref, dk_ref, dv_ref) = refs[8], refs[9:13], refs[13:]
    y, zl, core = (lax.axis_index(a) for a in ("y", "zl", "core"))
    for step in range(4):
        source = lax.rem(y - step + 4, 4)
        for line in range(4):
            all_ref[source, line, core] = own_refs[step][line]
            all_ref[source, line, 1 - core] = peer_refs[step][line]
    dk_ref[...] = jnp.zeros_like(dk_ref)
    dv_ref[...] = jnp.zeros_like(dv_ref)

    def put(place, part, value):
        value = value.reshape(4, 2, 32, 128)
        for c in range(2):
            d_ref[place, c, :, :, part * 128 : (part + 1) * 128] = value[:, c]

    def rows_of(place):
        return all_ref[place].reshape(256, 512)

    for i in range(4):
        query, grad = rows_of(i)[:, 0:128], rows_of(i)[:, 384:512]
        width = (i + 1) * 256
        keys = jnp.concatenate([rows_of(j)[:, 128:256] for j in range(i + 1)], axis=0)
        values = jnp.concatenate([rows_of(j)[:, 256:384] for j in range(i + 1)], axis=0)
        scores = lax.dot_general(query, keys, NT, preferred_element_type=F32) * SCALE
        q_pos = i * 256 + lax.broadcasted_iota(jnp.int32, (256, width), 0)
        k_pos = lax.broadcasted_iota(jnp.int32, (256, width), 1)
        scores = jnp.where(k_pos <= q_pos, scores, NEG)
        expd = jnp.exp(scores - jnp.max(scores, axis=1, keepdims=True))
        probs = expd * (1.0 / jnp.sum(expd, axis=1, keepdims=True))
        d_prob = lax.dot_general(grad, values, NT, preferred_element_type=F32)
        delta = jnp.sum(probs * d_prob, axis=1, keepdims=True)
        d_score = (probs * (d_prob - delta)).astype(BF16)
        low = probs.astype(BF16)
        put(i, 0, (jnp.dot(d_score, keys, preferred_element_type=F32) * SCALE).astype(BF16))
        dk_ref[0:width, :] += lax.dot_general(d_score, query, TN, preferred_element_type=F32)
        dv_ref[0:width, :] += lax.dot_general(low, grad, TN, preferred_element_type=F32)
    for i in range(4):
        put(i, 1, (dk_ref[i * 256 : (i + 1) * 256, :] * SCALE).astype(BF16))
        put(i, 2, dv_ref[i * 256 : (i + 1) * 256, :].astype(BF16))
    for step in range(4):
        back_refs[step][...] = d_ref[lax.rem(y + step, 4), core, zl]


def weight_grad_kernel(
    chunk0_ref, chunk1_ref, chunk2_ref, chunk3_ref, d_ref, late_ref,
    keep_ref, send_ref, made_ref,
):
    y, core = lax.axis_index("y"), lax.axis_index("core")
    chunks = (chunk0_ref, chunk1_ref, chunk2_ref, chunk3_ref)
    rows = jnp.concatenate([ref[...] for ref in chunks], axis=0)
    terms = jnp.concatenate(
        [d_ref[lax.rem(y - step + 4, 4), core].reshape(128, 384) for step in range(4)], axis=0
    )
    made_ref[...] = lax.dot_general(rows, terms, TN, preferred_element_type=F32).reshape(
        2, 256, 384
    )
    keep_ref[...] = made_ref[core]
    send_ref[...] = made_ref[1 - core].astype(BF16)


def join_kernel(keep_ref, got_ref, late_ref, out_ref):
    total = keep_ref[...] + got_ref[...].astype(F32)
    out_ref[...] = total.astype(BF16).reshape(16, 16, 384)


def other_half_kernel(
    back0_ref, back1_ref, back2_ref, back3_ref, wq_ref, wk_ref, wv_ref, rows_ref, send_ref
):
    y = lax.axis_index("y")
    for step, back_ref in enumerate((back0_ref, back1_ref, back2_ref, back3_ref)):
        rows_ref[lax.rem(y - step + 4, 4)] = back_ref[...]
    other = 1 - lax.axis_index("zh")
    send_ref[...] = back_project(rows_ref, (wq_ref, wk_ref, wv_ref), other).astype(BF16)


def own_half_kernel(rows_ref, wq_ref, wk_ref, wv_ref, keep_ref):
    keep_ref[...] = back_project(rows_ref, (wq_ref, wk_ref, wv_ref), lax.axis_index("zh"))


def back_project(rows_ref, w_refs, half):
    total = jnp.zeros((32, 1024), F32)
    features = pl.ds(pl.multiple_of(half * 1024, 1024), 1024)
    for part, w_ref in enumerate(w_refs):
        rows = jnp.concatenate(
            [rows_ref[head, :, part * 128 : (part + 1) * 128] for head in range(4)], axis=1
        )
        total = total + lax.dot_general(rows, w_ref[features, :], NT, preferred_element_type=F32)
    return total


def spread_kernel(ids_ref, keep_ref, got_ref, out_ref):
    for block in range(2):
        onehot = slots_of(ids_ref, block)
        rows = slice(block * SLOTS, (block + 1) * SLOTS)
        total = keep_ref[rows, :] + got_ref[rows, :].astype(F32)
        share = (total / jnp.sum(onehot, axis=1, keepdims=True)).astype(BF16)
        out_ref[block * 128 : (block + 1) * 128, :] = lax.dot_general(
            onehot.astype(BF16), share, TN, preferred_element_type=F32
        ).astype(BF16)


def sum_kernel(parts_ref, q_ref, k_ref, v_ref):
    for head in range(4):
        total = jnp.zeros((16, 384), F32)
        for dp in range(4):
            total = total + parts_ref[dp, head].astype(F32)
        for part, out_ref in enumerate((q_ref, k_ref, v_ref)):
            out_ref[:, head * 128 : (head + 1) * 128] = total[:, part * 128 : (part + 1) * 128]


def call(kernel, outs, ins, mib, flops, moved, scratch=()):
    spaces = {
        "v": VMEM,
        "h": pl.BlockSpec(memory_space=pltpu.HBM),
    }
    return pl.pallas_call(
        kernel,
        out_shape=tuple(jax.ShapeDtypeStruct(shape, dtype) for shape, dtype in outs),
        in_specs=[spaces[place] for place in ins],
        out_specs=tuple(VMEM for _ in outs),
        scratch_shapes=list(scratch),
        compiler_params=pltpu.CompilerParams(vmem_limit_bytes=mib << 20),
        cost_estimate=pl.CostEstimate(flops=flops, bytes_accessed=moved, transcendentals=0),
    )


def swap(x, axis):
    return lax.ppermute(x, axis, [(0, 1), (1, 0)])


def exchange(x, axes):
    return lax.all_to_all(x, axes, 0, 0, tiled=True)


def turn(x, axis, step):
    return lax.ppermute(x, axis, [(i, (i + step) % 4) for i in range(4)])


def body(byte_states, segment_ids, w_query, w_key, w_value, d_out):
    ids = segment_ids[0]
    weights = (w_query, w_key, w_value)

    with jax.named_scope("gather_line_cotangents"):
        grad = d_out[0]
        grads_line = [grad] + [turn(grad, "zl", step) for step in range(1, 4)]
    with jax.named_scope("pool"):
        (pooled_out,) = call(
            pool_kernel, [((8, 32, 1024), BF16)], "hh", 62, 10**7, 2 << 20,
            scratch=[
                pltpu.VMEM((2, 128), jnp.int32),
                pltpu.VMEM((256, 1024), BF16),
                pltpu.SemaphoreType.DMA((2,)),
            ],
        )(ids, byte_states[0])
    with jax.named_scope("gather_line_rows"):
        pooled_line = exchange(pooled_out, ("zl", "zh")).reshape(4, 2, 32, 1024)

    with jax.named_scope("project"):
        *packed, chunk = call(
            project_kernel,
            [((4, 32, 512), BF16)] * 4 + [((128, 512), BF16)],
            "v" * 8, 10, 8 * 10**8, 8 << 20, scratch=[pltpu.VMEM((4, 4, 32, 512), BF16)],
        )(pooled_line, *grads_line, *weights)

    with jax.named_scope("share_heads"):
        own = [packed[0]] + [turn(packed[step], "y", step) for step in range(1, 4)]
        peer = [swap(x, "core") for x in own]
    with jax.named_scope("share_chunk"):
        chunks = [chunk] + [turn(chunk, "y", step) for step in range(1, 4)]

    with jax.named_scope("attention"):
        d_rows, *back = call(
            attention_kernel,
            [((4, 2, 4, 32, 384), BF16)] + [((32, 384), BF16)] * 4,
            "v" * 8, 16, 2 * 10**9, 4 << 20,
            scratch=[
                pltpu.VMEM((4, 4, 2, 32, 512), BF16),
                pltpu.VMEM((1024, 128), F32),
                pltpu.VMEM((1024, 128), F32),
            ],
        )(*own, *peer)

    with jax.named_scope("return_rows"):
        back = [back[0]] + [turn(back[step], "y", step) for step in range(1, 4)]
    with jax.named_scope("back_project"):
        rows, send = call(
            other_half_kernel, [((4, 32, 384), BF16), ((32, 1024), BF16)],
            "v" * 7, 8, 4 * 10**8, 7 << 20,
        )(*back, *weights)
        got = swap(send, "zh")
        (keep,) = call(
            own_half_kernel, [((32, 1024), F32)], "v" * 4, 8, 4 * 10**8, 7 << 20
        )(rows, *weights)

    with jax.named_scope("weight_grads"):
        grad_keep, grad_send = call(
            weight_grad_kernel, [((256, 384), F32), ((256, 384), BF16)], "v" * 5 + "h", 10,
            4 * 10**8, 2 << 20, scratch=[pltpu.VMEM((2, 256, 384), F32)],
        )(*chunks, d_rows, rows)
        grad_got = swap(grad_send, "core")
    with jax.named_scope("sum_grads"):
        (partial,) = call(
            join_kernel, [((16, 16, 384), BF16)], "vvh", 4, 10**6, 1 << 20
        )(grad_keep, grad_got, keep)
        parts = exchange(partial, ("dp", "y")).reshape(4, 4, 16, 384)
        grads = call(sum_kernel, [((16, 512), F32)] * 3, "v", 4, 10**5, 1 << 20)(parts)

    with jax.named_scope("spread"):
        (d_bytes,) = call(
            spread_kernel, [((256, 1024), BF16)], "vvv", 4, 10**7, 1 << 20
        )(ids, keep, got)
    return (d_bytes[None], *grads)


def solution(mesh):
    fine = Mesh(
        np.asarray(mesh.devices).reshape(4, 4, 4, 2, 2), ("dp", "y", "zl", "core", "zh")
    )
    seq = ("y", "zl", "core")
    rows = P(("dp", *seq), "zh")
    return jax.shard_map(
        body,
        mesh=fine,
        in_specs=(
            P("dp", seq, "zh"),
            P("dp", seq, None),
            P(None, "zh"),
            P(None, "zh"),
            P(None, "zh"),
            P("dp", seq, "zh"),
        ),
        out_specs=(P("dp", seq, "zh"), rows, rows, rows),
        check_vma=False,
    )
```

```python
import math

import jax
import jax.numpy as jnp
import numpy as np
from jax import lax
from jax.experimental import pallas as pl
from jax.experimental.pallas import tpu as pltpu
from jax.sharding import Mesh, PartitionSpec as P

HEAD_DIM = 128
SLOTS = 16
SCALE = 1.0 / math.sqrt(HEAD_DIM)
NEG = -1e30
F32 = jnp.float32
BF16 = jnp.bfloat16
NT = (((1,), (1,)), ((), ()))
TN = (((0,), (0,)), ((), ()))

VMEM = pl.BlockSpec(memory_space=pltpu.VMEM)


def slots_of(ids_ref, block):
    slot = lax.broadcasted_iota(jnp.int32, (SLOTS, 128), 0)
    return (ids_ref[block : block + 1, :] == slot).astype(F32)


def pool_kernel(ids_hbm, bytes_hbm, pooled_ref, ids_ref, bytes_ref, sems):
    copies = [
        pltpu.make_async_copy(ids_hbm, ids_ref, sems.at[0]),
        pltpu.make_async_copy(bytes_hbm, bytes_ref, sems.at[1]),
    ]
    for copy in copies:
        copy.start()
    for copy in copies:
        copy.wait()
    for block in range(2):
        onehot = slots_of(ids_ref, block)
        sums = jnp.dot(
            onehot.astype(BF16),
            bytes_ref[block * 128 : (block + 1) * 128, :],
            preferred_element_type=F32,
        )
        mean = (sums / jnp.sum(onehot, axis=1, keepdims=True)).astype(BF16)
        pooled_ref[block * SLOTS : (block + 1) * SLOTS, :] = mean


def project_kernel(
    mine_ref, got_ref, grad_ref, wq_ref, wk_ref, wv_ref,
    out0_ref, out1_ref, out2_ref, out3_ref, part0_ref, part1_ref, part2_ref, part3_ref,
    rows_ref, heads_ref, parts_ref,
):
    y, zl, zh = (lax.axis_index(a) for a in ("y", "zl", "zh"))
    rows_ref[zh] = mine_ref[...]
    rows_ref[1 - zh] = got_ref[...]
    rows = jnp.concatenate([rows_ref[0], rows_ref[1]], axis=1)
    for part, w_ref in enumerate((wq_ref, wk_ref, wv_ref)):
        made = jnp.dot(rows, w_ref[...], preferred_element_type=F32).astype(BF16)
        for head in range(4):
            lanes = slice(head * 128, (head + 1) * 128)
            heads_ref[head, :, part * 128 : (part + 1) * 128] = made[:, lanes]
    for head in range(4):
        heads_ref[head, :, 384:512] = grad_ref[:, head * 128 : (head + 1) * 128]
    for dp in range(4):
        for place in range(4):
            first = (dp * 4 + place) * 128
            parts_ref[place, :, dp * 128 : (dp + 1) * 128] = rows[:, first : first + 128]
    for step, out_ref in enumerate((out0_ref, out1_ref, out2_ref, out3_ref)):
        out_ref[...] = heads_ref[lax.rem(zl + step, 4)]
    for step, out_ref in enumerate((part0_ref, part1_ref, part2_ref, part3_ref)):
        out_ref[...] = parts_ref[lax.rem(y + step, 4)]


def stack_kernel(*refs):
    for axis, inputs, out_ref in (("zl", refs[0:4], refs[8]), ("y", refs[4:8], refs[9])):
        here = lax.axis_index(axis)
        for step, in_ref in enumerate(inputs):
            out_ref[lax.rem(here - step + 4, 4)] = in_ref[...]


def fetch_kernel(late_ref, wq_hbm, wk_hbm, wv_hbm, wq_ref, wk_ref, wv_ref, sems):
    copies = [
        pltpu.make_async_copy(wq_hbm, wq_ref, sems.at[0]),
        pltpu.make_async_copy(wk_hbm, wk_ref, sems.at[1]),
        pltpu.make_async_copy(wv_hbm, wv_ref, sems.at[2]),
    ]
    for copy in copies:
        copy.start()
    for copy in copies:
        copy.wait()


def attention_kernel(*refs):
    own_refs, peer_refs = refs[0:4], refs[4:8]
    d_ref, back_refs, (all_ref, dk_ref, dv_ref) = refs[8], refs[9:13], refs[13:]
    y, zl, core = (lax.axis_index(a) for a in ("y", "zl", "core"))
    for step in range(4):
        source = lax.rem(y - step + 4, 4)
        for line in range(4):
            all_ref[source, line, core] = own_refs[step][line]
            all_ref[source, line, 1 - core] = peer_refs[step][line]
    dk_ref[...] = jnp.zeros_like(dk_ref)
    dv_ref[...] = jnp.zeros_like(dv_ref)

    def put(place, part, value):
        value = value.reshape(4, 2, 32, 128)
        for c in range(2):
            d_ref[place, c, :, :, part * 128 : (part + 1) * 128] = value[:, c]

    def rows_of(place):
        return all_ref[place].reshape(256, 512)

    for i in range(4):
        query, grad = rows_of(i)[:, 0:128], rows_of(i)[:, 384:512]
        width = (i + 1) * 256
        keys = jnp.concatenate([rows_of(j)[:, 128:256] for j in range(i + 1)], axis=0)
        values = jnp.concatenate([rows_of(j)[:, 256:384] for j in range(i + 1)], axis=0)
        scores = lax.dot_general(query, keys, NT, preferred_element_type=F32) * SCALE
        q_pos = i * 256 + lax.broadcasted_iota(jnp.int32, (256, width), 0)
        k_pos = lax.broadcasted_iota(jnp.int32, (256, width), 1)
        scores = jnp.where(k_pos <= q_pos, scores, NEG)
        expd = jnp.exp(scores - jnp.max(scores, axis=1, keepdims=True))
        probs = expd * (1.0 / jnp.sum(expd, axis=1, keepdims=True))
        d_prob = lax.dot_general(grad, values, NT, preferred_element_type=F32)
        delta = jnp.sum(probs * d_prob, axis=1, keepdims=True)
        d_score = (probs * (d_prob - delta)).astype(BF16)
        low = probs.astype(BF16)
        put(i, 0, (jnp.dot(d_score, keys, preferred_element_type=F32) * SCALE).astype(BF16))
        dk_ref[0:width, :] += lax.dot_general(d_score, query, TN, preferred_element_type=F32)
        dv_ref[0:width, :] += lax.dot_general(low, grad, TN, preferred_element_type=F32)
    for i in range(4):
        put(i, 1, (dk_ref[i * 256 : (i + 1) * 256, :] * SCALE).astype(BF16))
        put(i, 2, dv_ref[i * 256 : (i + 1) * 256, :].astype(BF16))
    for step in range(4):
        back_refs[step][...] = d_ref[y, core, lax.rem(zl + step, 4)]


def weight_grad_kernel(
    chunk0_ref, chunk1_ref, chunk2_ref, chunk3_ref, d_ref, late_ref,
    keep_ref, send_ref, made_ref,
):
    zl, core = lax.axis_index("zl"), lax.axis_index("core")
    chunks = (chunk0_ref, chunk1_ref, chunk2_ref, chunk3_ref)
    rows = jnp.concatenate([ref[...].reshape(128, 512) for ref in chunks], axis=0)
    terms = jnp.concatenate(
        [
            d_ref[place, core, lax.rem(zl - step + 4, 4)]
            for step in range(4)
            for place in range(4)
        ],
        axis=0,
    )
    made_ref[...] = lax.dot_general(rows, terms, TN, preferred_element_type=F32).reshape(
        16, 2, 16, 384
    )
    keep_ref[...] = made_ref[:, core]
    send_ref[...] = made_ref[:, 1 - core].astype(BF16)


def join_kernel(keep_ref, got_ref, late_ref, out_ref):
    out_ref[...] = (keep_ref[...] + got_ref[...].astype(F32)).astype(BF16)


def other_half_kernel(
    back0_ref, back1_ref, back2_ref, back3_ref, wq_ref, wk_ref, wv_ref, rows_ref, send_ref
):
    zl = lax.axis_index("zl")
    for step, back_ref in enumerate((back0_ref, back1_ref, back2_ref, back3_ref)):
        rows_ref[lax.rem(zl - step + 4, 4)] = back_ref[...]
    other = 1 - lax.axis_index("zh")
    send_ref[...] = back_project(rows_ref, (wq_ref, wk_ref, wv_ref), other).astype(BF16)


def own_half_kernel(rows_ref, wq_ref, wk_ref, wv_ref, keep_ref):
    keep_ref[...] = back_project(rows_ref, (wq_ref, wk_ref, wv_ref), lax.axis_index("zh"))


def back_project(rows_ref, w_refs, half):
    total = jnp.zeros((32, 1024), F32)
    features = pl.ds(pl.multiple_of(half * 1024, 1024), 1024)
    for part, w_ref in enumerate(w_refs):
        rows = jnp.concatenate(
            [rows_ref[head, :, part * 128 : (part + 1) * 128] for head in range(4)], axis=1
        )
        total = total + lax.dot_general(rows, w_ref[features, :], NT, preferred_element_type=F32)
    return total


def spread_kernel(ids_ref, keep_ref, got_ref, out_ref):
    for block in range(2):
        onehot = slots_of(ids_ref, block)
        rows = slice(block * SLOTS, (block + 1) * SLOTS)
        total = keep_ref[rows, :] + got_ref[rows, :].astype(F32)
        share = (total / jnp.sum(onehot, axis=1, keepdims=True)).astype(BF16)
        out_ref[block * 128 : (block + 1) * 128, :] = lax.dot_general(
            onehot.astype(BF16), share, TN, preferred_element_type=F32
        ).astype(BF16)


def sum_kernel(parts_ref, q_ref, k_ref, v_ref):
    for head in range(4):
        total = jnp.zeros((16, 384), F32)
        for dp in range(4):
            total = total + parts_ref[dp, head].astype(F32)
        for part, out_ref in enumerate((q_ref, k_ref, v_ref)):
            out_ref[:, head * 128 : (head + 1) * 128] = total[:, part * 128 : (part + 1) * 128]


def call(kernel, outs, ins, mib, flops, moved, scratch=()):
    spaces = {
        "v": VMEM,
        "h": pl.BlockSpec(memory_space=pltpu.HBM),
    }
    return pl.pallas_call(
        kernel,
        out_shape=tuple(jax.ShapeDtypeStruct(shape, dtype) for shape, dtype in outs),
        in_specs=[spaces[place] for place in ins],
        out_specs=tuple(VMEM for _ in outs),
        scratch_shapes=list(scratch),
        compiler_params=pltpu.CompilerParams(vmem_limit_bytes=mib << 20),
        cost_estimate=pl.CostEstimate(flops=flops, bytes_accessed=moved, transcendentals=0),
    )


def swap(x, axis):
    return lax.ppermute(x, axis, [(0, 1), (1, 0)])


def exchange(x, axes):
    return lax.all_to_all(x, axes, 0, 0, tiled=True)


def turn(x, axis, step):
    return lax.ppermute(x, axis, [(i, (i + step) % 4) for i in range(4)])


def body(byte_states, segment_ids, w_query, w_key, w_value, d_out):
    ids = segment_ids[0]
    weights = (w_query, w_key, w_value)

    with jax.named_scope("pool"):
        (pooled,) = call(
            pool_kernel, [((32, 1024), BF16)], "hh", 62, 10**7, 2 << 20,
            scratch=[
                pltpu.VMEM((2, 128), jnp.int32),
                pltpu.VMEM((256, 1024), BF16),
                pltpu.SemaphoreType.DMA((2,)),
            ],
        )(ids, byte_states[0])
    with jax.named_scope("share_features"):
        pooled_got = swap(pooled, "zh")
    with jax.named_scope("fetch_weights"):
        weights = call(
            fetch_kernel, [((2048, 512), BF16)] * 3, "hhhh", 4, 10**6, 12 << 20,
            scratch=[pltpu.SemaphoreType.DMA((3,))],
        )(pooled, *weights)

    with jax.named_scope("project"):
        made = call(
            project_kernel,
            [((32, 512), BF16)] * 8,
            "v" * 6, 10, 2 * 10**8, 8 << 20,
            scratch=[
                pltpu.VMEM((2, 32, 1024), BF16),
                pltpu.VMEM((4, 32, 512), BF16),
                pltpu.VMEM((4, 32, 512), BF16),
            ],
        )(pooled, pooled_got, d_out[0], *weights)
        heads, parts = made[:4], made[4:]

    with jax.named_scope("share_heads"):
        packed, chunk = call(
            stack_kernel, [((4, 32, 512), BF16)] * 2, "v" * 8, 4, 10**5, 1 << 19
        )(
            heads[0], *(turn(heads[step], "zl", step) for step in range(1, 4)),
            parts[0], *(turn(parts[step], "y", step) for step in range(1, 4)),
        )
        own = [packed] + [turn(packed, "y", step) for step in range(1, 4)]
        peer = [swap(x, "core") for x in own]
    with jax.named_scope("share_chunk"):
        chunks = [chunk] + [turn(chunk, "zl", step) for step in range(1, 4)]

    with jax.named_scope("attention"):
        d_rows, *back = call(
            attention_kernel,
            [((4, 2, 4, 32, 384), BF16)] + [((32, 384), BF16)] * 4,
            "v" * 8, 16, 2 * 10**9, 4 << 20,
            scratch=[
                pltpu.VMEM((4, 4, 2, 32, 512), BF16),
                pltpu.VMEM((1024, 128), F32),
                pltpu.VMEM((1024, 128), F32),
            ],
        )(*own, *peer)

    with jax.named_scope("return_rows"):
        back = [back[0]] + [turn(back[step], "zl", step) for step in range(1, 4)]
    with jax.named_scope("back_project"):
        rows, send = call(
            other_half_kernel, [((4, 32, 384), BF16), ((32, 1024), BF16)],
            "v" * 7, 8, 4 * 10**8, 7 << 20,
        )(*back, *weights)
        got = swap(send, "zh")
        (keep,) = call(
            own_half_kernel, [((32, 1024), F32)], "v" * 4, 8, 4 * 10**8, 7 << 20
        )(rows, *weights)

    with jax.named_scope("weight_grads"):
        grad_keep, grad_send = call(
            weight_grad_kernel, [((16, 16, 384), F32), ((16, 16, 384), BF16)], "v" * 5 + "h", 10,
            4 * 10**8, 2 << 20, scratch=[pltpu.VMEM((16, 2, 16, 384), F32)],
        )(*chunks, d_rows, rows)
        grad_got = swap(grad_send, "core")
    with jax.named_scope("sum_grads"):
        (partial,) = call(
            join_kernel, [((16, 16, 384), BF16)], "vvh", 4, 10**6, 1 << 20
        )(grad_keep, grad_got, keep)
        parts = exchange(partial, ("dp", "zl")).reshape(4, 4, 16, 384)
        grads = call(sum_kernel, [((16, 512), F32)] * 3, "v", 4, 10**5, 1 << 20)(parts)

    with jax.named_scope("spread"):
        (d_bytes,) = call(
            spread_kernel, [((256, 1024), BF16)], "vvv", 4, 10**7, 1 << 20
        )(ids, keep, got)
    return (d_bytes[None], *grads)


def solution(mesh):
    fine = Mesh(
        np.asarray(mesh.devices).reshape(4, 4, 4, 2, 2), ("dp", "y", "zl", "core", "zh")
    )
    seq = ("y", "zl", "core")
    rows = P(("dp", *seq), "zh")
    return jax.shard_map(
        body,
        mesh=fine,
        in_specs=(
            P("dp", seq, "zh"),
            P("dp", seq, None),
            P(None, "zh"),
            P(None, "zh"),
            P(None, "zh"),
            P("dp", seq, "zh"),
        ),
        out_specs=(P("dp", seq, "zh"), rows, rows, rows),
        check_vma=False,
    )
```

```python
import math

import jax
import jax.numpy as jnp
import numpy as np
from jax import lax
from jax.experimental import pallas as pl
from jax.experimental.pallas import tpu as pltpu
from jax.sharding import Mesh, PartitionSpec as P

HEAD_DIM = 128
SLOTS = 16
SCALE = 1.0 / math.sqrt(HEAD_DIM)
NEG = -1e30
F32 = jnp.float32
BF16 = jnp.bfloat16
NT = (((1,), (1,)), ((), ()))
TN = (((0,), (0,)), ((), ()))

VMEM = pl.BlockSpec(memory_space=pltpu.VMEM)


def slots_of(ids_ref, block):
    slot = lax.broadcasted_iota(jnp.int32, (SLOTS, 128), 0)
    return (ids_ref[block : block + 1, :] == slot).astype(F32)


def pool_kernel(ids_hbm, bytes_hbm, pooled_ref, ids_ref, bytes_ref, sems):
    copies = [
        pltpu.make_async_copy(ids_hbm, ids_ref, sems.at[0]),
        pltpu.make_async_copy(bytes_hbm, bytes_ref, sems.at[1]),
    ]
    for copy in copies:
        copy.start()
    for copy in copies:
        copy.wait()
    for block in range(2):
        onehot = slots_of(ids_ref, block)
        sums = jnp.dot(
            onehot.astype(BF16),
            bytes_ref[block * 128 : (block + 1) * 128, :],
            preferred_element_type=F32,
        )
        mean = (sums / jnp.sum(onehot, axis=1, keepdims=True)).astype(BF16)
        pooled_ref[block * SLOTS : (block + 1) * SLOTS, :] = mean


def project_kernel(
    mine_ref, got_ref, grad_ref, wq_ref, wk_ref, wv_ref,
    out0_ref, out1_ref, out2_ref, out3_ref, part0_ref, part1_ref, part2_ref, part3_ref,
    rows_ref, heads_ref, parts_ref,
):
    y, zl, zh = (lax.axis_index(a) for a in ("y", "zl", "zh"))
    rows_ref[zh] = mine_ref[...]
    rows_ref[1 - zh] = got_ref[...]
    rows = jnp.concatenate([rows_ref[0], rows_ref[1]], axis=1)
    for part, w_ref in enumerate((wq_ref, wk_ref, wv_ref)):
        made = jnp.dot(rows, w_ref[...], preferred_element_type=F32).astype(BF16)
        for head in range(4):
            lanes = slice(head * 128, (head + 1) * 128)
            heads_ref[head, :, part * 128 : (part + 1) * 128] = made[:, lanes]
    for head in range(4):
        heads_ref[head, :, 384:512] = grad_ref[:, head * 128 : (head + 1) * 128]
    for dp in range(4):
        for place in range(4):
            first = (dp * 4 + place) * 128
            parts_ref[place, :, dp * 128 : (dp + 1) * 128] = rows[:, first : first + 128]
    for step, out_ref in enumerate((out0_ref, out1_ref, out2_ref, out3_ref)):
        out_ref[...] = heads_ref[lax.rem(zl + step, 4)]
    for step, out_ref in enumerate((part0_ref, part1_ref, part2_ref, part3_ref)):
        out_ref[...] = parts_ref[lax.rem(y + step, 4)]


def stack_kernel(*refs):
    for axis, inputs, out_ref in (("zl", refs[0:4], refs[8]), ("y", refs[4:8], refs[9])):
        here = lax.axis_index(axis)
        for step, in_ref in enumerate(inputs):
            out_ref[lax.rem(here - step + 4, 4)] = in_ref[...]


def fetch_kernel(late_ref, wq_hbm, wk_hbm, wv_hbm, wq_ref, wk_ref, wv_ref, sems):
    copies = [
        pltpu.make_async_copy(wq_hbm, wq_ref, sems.at[0]),
        pltpu.make_async_copy(wk_hbm, wk_ref, sems.at[1]),
        pltpu.make_async_copy(wv_hbm, wv_ref, sems.at[2]),
    ]
    for copy in copies:
        copy.start()
    for copy in copies:
        copy.wait()


def attention_kernel(*refs):
    own_refs, peer_refs = refs[0:4], refs[4:8]
    d_ref, back_refs, (all_ref, dk_ref, dv_ref) = refs[8], refs[9:13], refs[13:]
    y, zl, core = (lax.axis_index(a) for a in ("y", "zl", "core"))
    for step in range(4):
        source = lax.rem(y - step + 4, 4)
        for line in range(4):
            all_ref[source, line, core] = own_refs[step][line]
            all_ref[source, line, 1 - core] = peer_refs[step][line]
    dk_ref[...] = jnp.zeros_like(dk_ref)
    dv_ref[...] = jnp.zeros_like(dv_ref)

    def put(place, part, value):
        value = value.reshape(4, 2, 32, 128)
        for c in range(2):
            d_ref[place, c, :, :, part * 128 : (part + 1) * 128] = value[:, c]

    def rows_of(place):
        return all_ref[place].reshape(256, 512)

    for i in range(4):
        query, grad = rows_of(i)[:, 0:128], rows_of(i)[:, 384:512]
        width = (i + 1) * 256
        keys = jnp.concatenate([rows_of(j)[:, 128:256] for j in range(i + 1)], axis=0)
        values = jnp.concatenate([rows_of(j)[:, 256:384] for j in range(i + 1)], axis=0)
        scores = lax.dot_general(query, keys, NT, preferred_element_type=F32) * SCALE
        q_pos = i * 256 + lax.broadcasted_iota(jnp.int32, (256, width), 0)
        k_pos = lax.broadcasted_iota(jnp.int32, (256, width), 1)
        scores = jnp.where(k_pos <= q_pos, scores, NEG)
        expd = jnp.exp(scores - jnp.max(scores, axis=1, keepdims=True))
        probs = expd * (1.0 / jnp.sum(expd, axis=1, keepdims=True))
        d_prob = lax.dot_general(grad, values, NT, preferred_element_type=F32)
        delta = jnp.sum(probs * d_prob, axis=1, keepdims=True)
        d_score = (probs * (d_prob - delta)).astype(BF16)
        low = probs.astype(BF16)
        put(i, 0, (jnp.dot(d_score, keys, preferred_element_type=F32) * SCALE).astype(BF16))
        dk_ref[0:width, :] += lax.dot_general(d_score, query, TN, preferred_element_type=F32)
        dv_ref[0:width, :] += lax.dot_general(low, grad, TN, preferred_element_type=F32)
    for i in range(4):
        put(i, 1, (dk_ref[i * 256 : (i + 1) * 256, :] * SCALE).astype(BF16))
        put(i, 2, dv_ref[i * 256 : (i + 1) * 256, :].astype(BF16))
    for step in range(4):
        back_refs[step][...] = d_ref[y, core, lax.rem(zl + step, 4)]


def weight_grad_kernel(
    chunk0_ref, chunk1_ref, chunk2_ref, chunk3_ref, d_ref, late_ref,
    keep_ref, send_ref, made_ref,
):
    zl, core = lax.axis_index("zl"), lax.axis_index("core")
    chunks = (chunk0_ref, chunk1_ref, chunk2_ref, chunk3_ref)
    rows = jnp.concatenate([ref[...].reshape(128, 512) for ref in chunks], axis=0)
    terms = jnp.concatenate(
        [
            d_ref[place, core, lax.rem(zl - step + 4, 4)]
            for step in range(4)
            for place in range(4)
        ],
        axis=0,
    )
    made_ref[...] = lax.dot_general(rows, terms, TN, preferred_element_type=F32).reshape(
        16, 2, 16, 384
    )
    keep_ref[...] = made_ref[:, core]
    send_ref[...] = made_ref[:, 1 - core].astype(BF16)


def join_kernel(keep_ref, got_ref, late0_ref, late1_ref, out_ref):
    out_ref[...] = (keep_ref[...] + got_ref[...].astype(F32)).astype(BF16)


def other_half_kernel(
    back0_ref, back1_ref, back2_ref, back3_ref, wq_ref, wk_ref, wv_ref, rows_ref, send_ref
):
    zl = lax.axis_index("zl")
    for step, back_ref in enumerate((back0_ref, back1_ref, back2_ref, back3_ref)):
        rows_ref[lax.rem(zl - step + 4, 4)] = back_ref[...]
    other = 1 - lax.axis_index("zh")
    send_ref[...] = back_project(rows_ref, (wq_ref, wk_ref, wv_ref), other).astype(BF16)


def own_half_kernel(rows_ref, wq_ref, wk_ref, wv_ref, keep_ref):
    keep_ref[...] = back_project(rows_ref, (wq_ref, wk_ref, wv_ref), lax.axis_index("zh"))


def back_project(rows_ref, w_refs, half):
    total = jnp.zeros((32, 1024), F32)
    features = pl.ds(pl.multiple_of(half * 1024, 1024), 1024)
    for part, w_ref in enumerate(w_refs):
        rows = jnp.concatenate(
            [rows_ref[head, :, part * 128 : (part + 1) * 128] for head in range(4)], axis=1
        )
        total = total + lax.dot_general(rows, w_ref[features, :], NT, preferred_element_type=F32)
    return total


def spread_kernel(ids_ref, keep_ref, got_ref, out_ref):
    for block in range(2):
        onehot = slots_of(ids_ref, block)
        rows = slice(block * SLOTS, (block + 1) * SLOTS)
        total = keep_ref[rows, :] + got_ref[rows, :].astype(F32)
        share = (total / jnp.sum(onehot, axis=1, keepdims=True)).astype(BF16)
        out_ref[block * 128 : (block + 1) * 128, :] = lax.dot_general(
            onehot.astype(BF16), share, TN, preferred_element_type=F32
        ).astype(BF16)


def sum_kernel(parts_ref, q_ref, k_ref, v_ref):
    for head in range(4):
        total = jnp.zeros((16, 384), F32)
        for dp in range(4):
            total = total + parts_ref[dp, head].astype(F32)
        for part, out_ref in enumerate((q_ref, k_ref, v_ref)):
            out_ref[:, head * 128 : (head + 1) * 128] = total[:, part * 128 : (part + 1) * 128]


def call(kernel, outs, ins, mib, flops, moved, scratch=()):
    spaces = {
        "v": VMEM,
        "h": pl.BlockSpec(memory_space=pltpu.HBM),
    }
    return pl.pallas_call(
        kernel,
        out_shape=tuple(jax.ShapeDtypeStruct(shape, dtype) for shape, dtype in outs),
        in_specs=[spaces[place] for place in ins],
        out_specs=tuple(VMEM for _ in outs),
        scratch_shapes=list(scratch),
        compiler_params=pltpu.CompilerParams(vmem_limit_bytes=mib << 20),
        cost_estimate=pl.CostEstimate(flops=flops, bytes_accessed=moved, transcendentals=0),
    )


def swap(x, axis):
    return lax.ppermute(x, axis, [(0, 1), (1, 0)])


def exchange(x, axes):
    return lax.all_to_all(x, axes, 0, 0, tiled=True)


def turn(x, axis, step):
    return lax.ppermute(x, axis, [(i, (i + step) % 4) for i in range(4)])


def body(byte_states, segment_ids, w_query, w_key, w_value, d_out):
    ids = segment_ids[0]
    weights = (w_query, w_key, w_value)

    with jax.named_scope("pool"):
        (pooled,) = call(
            pool_kernel, [((32, 1024), BF16)], "hh", 62, 10**7, 2 << 20,
            scratch=[
                pltpu.VMEM((2, 128), jnp.int32),
                pltpu.VMEM((256, 1024), BF16),
                pltpu.SemaphoreType.DMA((2,)),
            ],
        )(ids, byte_states[0])
    with jax.named_scope("share_features"):
        pooled_got = swap(pooled, "zh")
    with jax.named_scope("fetch_weights"):
        weights = call(
            fetch_kernel, [((2048, 512), BF16)] * 3, "hhhh", 4, 10**6, 12 << 20,
            scratch=[pltpu.SemaphoreType.DMA((3,))],
        )(pooled, *weights)

    with jax.named_scope("project"):
        made = call(
            project_kernel,
            [((32, 512), BF16)] * 8,
            "v" * 6, 10, 2 * 10**8, 8 << 20,
            scratch=[
                pltpu.VMEM((2, 32, 1024), BF16),
                pltpu.VMEM((4, 32, 512), BF16),
                pltpu.VMEM((4, 32, 512), BF16),
            ],
        )(pooled, pooled_got, d_out[0], *weights)
        heads, parts = made[:4], made[4:]

    with jax.named_scope("share_heads"):
        packed, chunk = call(
            stack_kernel, [((4, 32, 512), BF16)] * 2, "v" * 8, 4, 10**5, 1 << 19
        )(
            heads[0], *(turn(heads[step], "zl", step) for step in range(1, 4)),
            parts[0], *(turn(parts[step], "y", step) for step in range(1, 4)),
        )
        own = [packed] + [turn(packed, "y", step) for step in range(1, 4)]
        peer = [swap(x, "core") for x in own]
    with jax.named_scope("share_chunk"):
        chunks = [chunk] + [turn(chunk, "zl", step) for step in range(1, 4)]

    with jax.named_scope("attention"):
        d_rows, *back = call(
            attention_kernel,
            [((4, 2, 4, 32, 384), BF16)] + [((32, 384), BF16)] * 4,
            "v" * 8, 16, 2 * 10**9, 4 << 20,
            scratch=[
                pltpu.VMEM((4, 4, 2, 32, 512), BF16),
                pltpu.VMEM((1024, 128), F32),
                pltpu.VMEM((1024, 128), F32),
            ],
        )(*own, *peer)

    with jax.named_scope("return_rows"):
        back = [back[0]] + [turn(back[step], "zl", step) for step in range(1, 4)]
    with jax.named_scope("back_project"):
        rows, send = call(
            other_half_kernel, [((4, 32, 384), BF16), ((32, 1024), BF16)],
            "v" * 7, 8, 4 * 10**8, 7 << 20,
        )(*back, *weights)
        got = swap(send, "zh")
        (keep,) = call(
            own_half_kernel, [((32, 1024), F32)], "v" * 4, 8, 4 * 10**8, 7 << 20
        )(rows, *weights)

    with jax.named_scope("weight_grads"):
        grad_keep, grad_send = call(
            weight_grad_kernel, [((16, 16, 384), F32), ((16, 16, 384), BF16)], "v" * 5 + "h", 10,
            4 * 10**8, 2 << 20, scratch=[pltpu.VMEM((16, 2, 16, 384), F32)],
        )(*chunks, d_rows, rows)
        grad_got = swap(grad_send, "core")
    with jax.named_scope("sum_grads"):
        (partial,) = call(
            join_kernel, [((16, 16, 384), BF16)], "vvhh", 4, 10**6, 1 << 20
        )(grad_keep, grad_got, keep, got)
        parts = exchange(partial, ("dp", "zl")).reshape(4, 4, 16, 384)
        grads = call(sum_kernel, [((16, 512), F32)] * 3, "v", 4, 10**5, 1 << 20)(parts)

    with jax.named_scope("spread"):
        (d_bytes,) = call(
            spread_kernel, [((256, 1024), BF16)], "vvv", 4, 10**7, 1 << 20
        )(ids, keep, got)
    return (d_bytes[None], *grads)


def solution(mesh):
    fine = Mesh(
        np.asarray(mesh.devices).reshape(4, 4, 4, 2, 2), ("dp", "y", "zl", "core", "zh")
    )
    seq = ("y", "zl", "core")
    rows = P(("dp", *seq), "zh")
    return jax.shard_map(
        body,
        mesh=fine,
        in_specs=(
            P("dp", seq, "zh"),
            P("dp", seq, None),
            P(None, "zh"),
            P(None, "zh"),
            P(None, "zh"),
            P("dp", seq, "zh"),
        ),
        out_specs=(P("dp", seq, "zh"), rows, rows, rows),
        check_vma=False,
    )
```

```python
import math

import jax
import jax.numpy as jnp
import numpy as np
from jax import lax
from jax.experimental import pallas as pl
from jax.experimental.pallas import tpu as pltpu
from jax.sharding import Mesh, PartitionSpec as P

HEAD_DIM = 128
SLOTS = 16
SCALE = 1.0 / math.sqrt(HEAD_DIM)
NEG = -1e30
F32 = jnp.float32
BF16 = jnp.bfloat16
NT = (((1,), (1,)), ((), ()))
TN = (((0,), (0,)), ((), ()))

VMEM = pl.BlockSpec(memory_space=pltpu.VMEM)


def slots_of(ids_ref, block):
    slot = lax.broadcasted_iota(jnp.int32, (SLOTS, 128), 0)
    return (ids_ref[block : block + 1, :] == slot).astype(F32)


def pool_kernel(ids_hbm, bytes_hbm, pooled_ref, ids_ref, bytes_ref, sems):
    copies = [
        pltpu.make_async_copy(ids_hbm, ids_ref, sems.at[0]),
        pltpu.make_async_copy(bytes_hbm, bytes_ref, sems.at[1]),
    ]
    for copy in copies:
        copy.start()
    for copy in copies:
        copy.wait()
    for block in range(2):
        onehot = slots_of(ids_ref, block)
        sums = jnp.dot(
            onehot.astype(BF16),
            bytes_ref[block * 128 : (block + 1) * 128, :],
            preferred_element_type=F32,
        )
        mean = (sums / jnp.sum(onehot, axis=1, keepdims=True)).astype(BF16)
        pooled_ref[block * SLOTS : (block + 1) * SLOTS, :] = mean


def project_kernel(
    mine_ref, got_ref, grad_ref, wq_ref, wk_ref, wv_ref,
    out0_ref, out1_ref, out2_ref, out3_ref, part0_ref, part1_ref, part2_ref, part3_ref,
    rows_ref, heads_ref, parts_ref,
):
    y, zl, zh = (lax.axis_index(a) for a in ("y", "zl", "zh"))
    rows_ref[zh] = mine_ref[...]
    rows_ref[1 - zh] = got_ref[...]
    rows = jnp.concatenate([rows_ref[0], rows_ref[1]], axis=1)
    for part, w_ref in enumerate((wq_ref, wk_ref, wv_ref)):
        made = jnp.dot(rows, w_ref[...], preferred_element_type=F32).astype(BF16)
        for head in range(4):
            lanes = slice(head * 128, (head + 1) * 128)
            heads_ref[head, :, part * 128 : (part + 1) * 128] = made[:, lanes]
    for head in range(4):
        heads_ref[head, :, 384:512] = grad_ref[:, head * 128 : (head + 1) * 128]
    for dp in range(4):
        for place in range(4):
            first = (dp * 4 + place) * 128
            parts_ref[place, :, dp * 128 : (dp + 1) * 128] = rows[:, first : first + 128]
    for step, out_ref in enumerate((out0_ref, out1_ref, out2_ref, out3_ref)):
        out_ref[...] = heads_ref[lax.rem(zl + step, 4)]
    for step, out_ref in enumerate((part0_ref, part1_ref, part2_ref, part3_ref)):
        out_ref[...] = parts_ref[lax.rem(y + step, 4)]


def stack_kernel(*refs):
    for axis, inputs, out_ref in (("zl", refs[0:4], refs[8]), ("y", refs[4:8], refs[9])):
        here = lax.axis_index(axis)
        for step, in_ref in enumerate(inputs):
            out_ref[lax.rem(here - step + 4, 4)] = in_ref[...]


def fetch_kernel(wq_hbm, wk_hbm, wv_hbm, wq_ref, wk_ref, wv_ref, sems):
    copies = [
        pltpu.make_async_copy(wq_hbm, wq_ref, sems.at[0]),
        pltpu.make_async_copy(wk_hbm, wk_ref, sems.at[1]),
        pltpu.make_async_copy(wv_hbm, wv_ref, sems.at[2]),
    ]
    for copy in copies:
        copy.start()
    for copy in copies:
        copy.wait()


def attention_kernel(*refs):
    own_refs, peer_refs = refs[0:4], refs[4:8]
    d_ref, back_refs, (all_ref, dk_ref, dv_ref) = refs[8], refs[9:13], refs[13:]
    y, zl, core = (lax.axis_index(a) for a in ("y", "zl", "core"))
    for step in range(4):
        source = lax.rem(y - step + 4, 4)
        for line in range(4):
            all_ref[source, line, core] = own_refs[step][line]
            all_ref[source, line, 1 - core] = peer_refs[step][line]
    dk_ref[...] = jnp.zeros_like(dk_ref)
    dv_ref[...] = jnp.zeros_like(dv_ref)

    def put(place, part, value):
        value = value.reshape(4, 2, 32, 128)
        for c in range(2):
            d_ref[place, c, :, :, part * 128 : (part + 1) * 128] = value[:, c]

    def rows_of(place):
        return all_ref[place].reshape(256, 512)

    for i in range(4):
        query, grad = rows_of(i)[:, 0:128], rows_of(i)[:, 384:512]
        width = (i + 1) * 256
        keys = jnp.concatenate([rows_of(j)[:, 128:256] for j in range(i + 1)], axis=0)
        values = jnp.concatenate([rows_of(j)[:, 256:384] for j in range(i + 1)], axis=0)
        scores = lax.dot_general(query, keys, NT, preferred_element_type=F32) * SCALE
        q_pos = i * 256 + lax.broadcasted_iota(jnp.int32, (256, width), 0)
        k_pos = lax.broadcasted_iota(jnp.int32, (256, width), 1)
        scores = jnp.where(k_pos <= q_pos, scores, NEG)
        expd = jnp.exp(scores - jnp.max(scores, axis=1, keepdims=True))
        probs = expd * (1.0 / jnp.sum(expd, axis=1, keepdims=True))
        d_prob = lax.dot_general(grad, values, NT, preferred_element_type=F32)
        delta = jnp.sum(probs * d_prob, axis=1, keepdims=True)
        d_score = (probs * (d_prob - delta)).astype(BF16)
        low = probs.astype(BF16)
        put(i, 0, (jnp.dot(d_score, keys, preferred_element_type=F32) * SCALE).astype(BF16))
        dk_ref[0:width, :] += lax.dot_general(d_score, query, TN, preferred_element_type=F32)
        dv_ref[0:width, :] += lax.dot_general(low, grad, TN, preferred_element_type=F32)
    for i in range(4):
        put(i, 1, (dk_ref[i * 256 : (i + 1) * 256, :] * SCALE).astype(BF16))
        put(i, 2, dv_ref[i * 256 : (i + 1) * 256, :].astype(BF16))
    for step in range(4):
        back_refs[step][...] = d_ref[y, core, lax.rem(zl + step, 4)]


def weight_grad_kernel(
    chunk0_ref, chunk1_ref, chunk2_ref, chunk3_ref, d_ref, late_ref,
    keep_ref, send_ref, made_ref,
):
    zl, core = lax.axis_index("zl"), lax.axis_index("core")
    chunks = (chunk0_ref, chunk1_ref, chunk2_ref, chunk3_ref)
    rows = jnp.concatenate([ref[...].reshape(128, 512) for ref in chunks], axis=0)
    terms = jnp.concatenate(
        [
            d_ref[place, core, lax.rem(zl - step + 4, 4)]
            for step in range(4)
            for place in range(4)
        ],
        axis=0,
    )
    made_ref[...] = lax.dot_general(rows, terms, TN, preferred_element_type=F32).reshape(
        16, 2, 16, 384
    )
    keep_ref[...] = made_ref[:, core]
    send_ref[...] = made_ref[:, 1 - core].astype(BF16)


def join_kernel(keep_ref, got_ref, late_ref, out_ref):
    out_ref[...] = (keep_ref[...] + got_ref[...].astype(F32)).astype(BF16)


def other_half_kernel(
    back0_ref, back1_ref, back2_ref, back3_ref, wq_ref, wk_ref, wv_ref, rows_ref, send_ref
):
    zl = lax.axis_index("zl")
    for step, back_ref in enumerate((back0_ref, back1_ref, back2_ref, back3_ref)):
        rows_ref[lax.rem(zl - step + 4, 4)] = back_ref[...]
    other = 1 - lax.axis_index("zh")
    send_ref[...] = back_project(rows_ref, (wq_ref, wk_ref, wv_ref), other).astype(BF16)


def own_half_kernel(rows_ref, wq_ref, wk_ref, wv_ref, keep_ref):
    keep_ref[...] = back_project(rows_ref, (wq_ref, wk_ref, wv_ref), lax.axis_index("zh"))


def back_project(rows_ref, w_refs, half):
    total = jnp.zeros((32, 1024), F32)
    features = pl.ds(pl.multiple_of(half * 1024, 1024), 1024)
    for part, w_ref in enumerate(w_refs):
        rows = jnp.concatenate(
            [rows_ref[head, :, part * 128 : (part + 1) * 128] for head in range(4)], axis=1
        )
        total = total + lax.dot_general(rows, w_ref[features, :], NT, preferred_element_type=F32)
    return total


def spread_kernel(ids_ref, keep_ref, got_ref, out_ref):
    for block in range(2):
        onehot = slots_of(ids_ref, block)
        rows = slice(block * SLOTS, (block + 1) * SLOTS)
        total = keep_ref[rows, :] + got_ref[rows, :].astype(F32)
        share = (total / jnp.sum(onehot, axis=1, keepdims=True)).astype(BF16)
        out_ref[block * 128 : (block + 1) * 128, :] = lax.dot_general(
            onehot.astype(BF16), share, TN, preferred_element_type=F32
        ).astype(BF16)


def sum_kernel(parts_ref, out0_ref, out1_ref, out2_ref, out3_ref, total_ref):
    zl = lax.axis_index("zl")
    for place in range(4):
        total = parts_ref[0, place].astype(F32)
        for dp in range(1, 4):
            total = total + parts_ref[dp, place].astype(F32)
        total_ref[place] = total
    for step, out_ref in enumerate((out0_ref, out1_ref, out2_ref, out3_ref)):
        out_ref[...] = total_ref[lax.rem(zl + step, 4)]


def place_kernel(in0_ref, in1_ref, in2_ref, in3_ref, q_ref, k_ref, v_ref, total_ref):
    zl = lax.axis_index("zl")
    for step, in_ref in enumerate((in0_ref, in1_ref, in2_ref, in3_ref)):
        total_ref[lax.rem(zl - step + 4, 4)] = in_ref[...]
    for head in range(4):
        for part, out_ref in enumerate((q_ref, k_ref, v_ref)):
            lanes = slice(part * 128, (part + 1) * 128)
            out_ref[:, head * 128 : (head + 1) * 128] = total_ref[head, :, lanes]


def call(kernel, outs, ins, mib, flops, moved, scratch=()):
    spaces = {
        "v": VMEM,
        "h": pl.BlockSpec(memory_space=pltpu.HBM),
    }
    return pl.pallas_call(
        kernel,
        out_shape=tuple(jax.ShapeDtypeStruct(shape, dtype) for shape, dtype in outs),
        in_specs=[spaces[place] for place in ins],
        out_specs=tuple(VMEM for _ in outs),
        scratch_shapes=list(scratch),
        compiler_params=pltpu.CompilerParams(vmem_limit_bytes=mib << 20),
        cost_estimate=pl.CostEstimate(flops=flops, bytes_accessed=moved, transcendentals=0),
    )


def swap(x, axis):
    return lax.ppermute(x, axis, [(0, 1), (1, 0)])


def exchange(x, axes):
    return lax.all_to_all(x, axes, 0, 0, tiled=True)


def turn(x, axis, step):
    return lax.ppermute(x, axis, [(i, (i + step) % 4) for i in range(4)])


def body(byte_states, segment_ids, w_query, w_key, w_value, d_out):
    ids = segment_ids[0]
    weights = (w_query, w_key, w_value)

    with jax.named_scope("pool"):
        (pooled,) = call(
            pool_kernel, [((32, 1024), BF16)], "hh", 62, 10**7, 2 << 20,
            scratch=[
                pltpu.VMEM((2, 128), jnp.int32),
                pltpu.VMEM((256, 1024), BF16),
                pltpu.SemaphoreType.DMA((2,)),
            ],
        )(ids, byte_states[0])
    with jax.named_scope("share_features"):
        pooled_got = swap(pooled, "zh")
    with jax.named_scope("fetch_weights"):
        *weights, _ = lax.optimization_barrier((*weights, pooled))
        weights = call(
            fetch_kernel, [((2048, 512), BF16)] * 3, "hhh", 4, 10**6, 12 << 20,
            scratch=[pltpu.SemaphoreType.DMA((3,))],
        )(*weights)

    with jax.named_scope("project"):
        made = call(
            project_kernel,
            [((32, 512), BF16)] * 8,
            "v" * 6, 10, 2 * 10**8, 8 << 20,
            scratch=[
                pltpu.VMEM((2, 32, 1024), BF16),
                pltpu.VMEM((4, 32, 512), BF16),
                pltpu.VMEM((4, 32, 512), BF16),
            ],
        )(pooled, pooled_got, d_out[0], *weights)
        heads, parts = made[:4], made[4:]

    with jax.named_scope("share_heads"):
        packed, chunk = call(
            stack_kernel, [((4, 32, 512), BF16)] * 2, "v" * 8, 4, 10**5, 1 << 19
        )(
            heads[0], *(turn(heads[step], "zl", step) for step in range(1, 4)),
            parts[0], *(turn(parts[step], "y", step) for step in range(1, 4)),
        )
        own = [packed] + [turn(packed, "y", step) for step in range(1, 4)]
        peer = [swap(x, "core") for x in own]
    with jax.named_scope("share_chunk"):
        chunks = [chunk] + [turn(chunk, "zl", step) for step in range(1, 4)]

    with jax.named_scope("attention"):
        d_rows, *back = call(
            attention_kernel,
            [((4, 2, 4, 32, 384), BF16)] + [((32, 384), BF16)] * 4,
            "v" * 8, 16, 2 * 10**9, 4 << 20,
            scratch=[
                pltpu.VMEM((4, 4, 2, 32, 512), BF16),
                pltpu.VMEM((1024, 128), F32),
                pltpu.VMEM((1024, 128), F32),
            ],
        )(*own, *peer)

    with jax.named_scope("return_rows"):
        back = [back[0]] + [turn(back[step], "zl", step) for step in range(1, 4)]
    with jax.named_scope("back_project"):
        rows, send = call(
            other_half_kernel, [((4, 32, 384), BF16), ((32, 1024), BF16)],
            "v" * 7, 8, 4 * 10**8, 7 << 20,
        )(*back, *weights)
        got = swap(send, "zh")
        (keep,) = call(
            own_half_kernel, [((32, 1024), F32)], "v" * 4, 8, 4 * 10**8, 7 << 20
        )(rows, *weights)

    with jax.named_scope("weight_grads"):
        grad_keep, grad_send = call(
            weight_grad_kernel, [((16, 16, 384), F32), ((16, 16, 384), BF16)], "v" * 5 + "h", 10,
            4 * 10**8, 2 << 20, scratch=[pltpu.VMEM((16, 2, 16, 384), F32)],
        )(*chunks, d_rows, rows)
        grad_got = swap(grad_send, "core")
    with jax.named_scope("sum_grads"):
        (partial,) = call(
            join_kernel, [((16, 16, 384), BF16)], "vvh", 4, 10**6, 1 << 20
        )(grad_keep, grad_got, keep)
        parts = exchange(partial.reshape(4, 4, 16, 384), "dp")
        scratch = [pltpu.VMEM((4, 16, 384), F32)]
        sums = call(
            sum_kernel, [((16, 384), F32)] * 4, "v", 4, 10**5, 1 << 20, scratch=scratch
        )(parts)
        sums = [sums[0]] + [turn(sums[step], "zl", step) for step in range(1, 4)]
        grads = call(
            place_kernel, [((16, 512), F32)] * 3, "vvvv", 4, 10**5, 1 << 20, scratch=scratch
        )(*sums)

    with jax.named_scope("spread"):
        (d_bytes,) = call(
            spread_kernel, [((256, 1024), BF16)], "vvv", 4, 10**7, 1 << 20
        )(ids, keep, got)
    return (d_bytes[None], *grads)


def solution(mesh):
    fine = Mesh(
        np.asarray(mesh.devices).reshape(4, 4, 4, 2, 2), ("dp", "y", "zl", "core", "zh")
    )
    seq = ("y", "zl", "core")
    rows = P(("dp", *seq), "zh")
    return jax.shard_map(
        body,
        mesh=fine,
        in_specs=(
            P("dp", seq, "zh"),
            P("dp", seq, None),
            P(None, "zh"),
            P(None, "zh"),
            P(None, "zh"),
            P("dp", seq, "zh"),
        ),
        out_specs=(P("dp", seq, "zh"), rows, rows, rows),
        check_vma=False,
    )
```

```python
import math

import jax
import jax.numpy as jnp
import numpy as np
from jax import lax
from jax.experimental import pallas as pl
from jax.experimental.pallas import tpu as pltpu
from jax.sharding import Mesh, PartitionSpec as P

HEAD_DIM = 128
SLOTS = 16
SCALE = 1.0 / math.sqrt(HEAD_DIM)
NEG = -1e30
F32 = jnp.float32
BF16 = jnp.bfloat16
NT = (((1,), (1,)), ((), ()))
TN = (((0,), (0,)), ((), ()))

VMEM = pl.BlockSpec(memory_space=pltpu.VMEM)


def slots_of(ids_ref, block):
    slot = lax.broadcasted_iota(jnp.int32, (SLOTS, 128), 0)
    return (ids_ref[block : block + 1, :] == slot).astype(F32)


def pool_kernel(ids_hbm, bytes_hbm, pooled_ref, ids_ref, bytes_ref, sems):
    copies = [
        pltpu.make_async_copy(ids_hbm, ids_ref, sems.at[0]),
        pltpu.make_async_copy(bytes_hbm, bytes_ref, sems.at[1]),
    ]
    for copy in copies:
        copy.start()
    for copy in copies:
        copy.wait()
    for block in range(2):
        onehot = slots_of(ids_ref, block)
        sums = jnp.dot(
            onehot.astype(BF16),
            bytes_ref[block * 128 : (block + 1) * 128, :],
            preferred_element_type=F32,
        )
        mean = (sums / jnp.sum(onehot, axis=1, keepdims=True)).astype(BF16)
        pooled_ref[block * SLOTS : (block + 1) * SLOTS, :] = mean


def project_kernel(
    mine_ref, got_ref, grad_ref, wq_ref, wk_ref, wv_ref,
    out0_ref, out1_ref, out2_ref, out3_ref, part0_ref, part1_ref, part2_ref, part3_ref,
    rows_ref, heads_ref, parts_ref,
):
    y, zl, zh = (lax.axis_index(a) for a in ("y", "zl", "zh"))
    rows_ref[zh] = mine_ref[...]
    rows_ref[1 - zh] = got_ref[...]
    rows = jnp.concatenate([rows_ref[0], rows_ref[1]], axis=1)
    for part, w_ref in enumerate((wq_ref, wk_ref, wv_ref)):
        made = jnp.dot(rows, w_ref[...], preferred_element_type=F32).astype(BF16)
        for head in range(4):
            lanes = slice(head * 128, (head + 1) * 128)
            heads_ref[head, :, part * 128 : (part + 1) * 128] = made[:, lanes]
    for head in range(4):
        heads_ref[head, :, 384:512] = grad_ref[:, head * 128 : (head + 1) * 128]
    for dp in range(4):
        for place in range(4):
            first = (dp * 4 + place) * 128
            parts_ref[place, :, dp * 128 : (dp + 1) * 128] = rows[:, first : first + 128]
    for step, out_ref in enumerate((out0_ref, out1_ref, out2_ref, out3_ref)):
        out_ref[...] = heads_ref[lax.rem(zl + step, 4)]
    for step, out_ref in enumerate((part0_ref, part1_ref, part2_ref, part3_ref)):
        out_ref[...] = parts_ref[lax.rem(y + step, 4)]


def stack_kernel(*refs):
    for axis, inputs, out_ref in (("zl", refs[0:4], refs[8]), ("y", refs[4:8], refs[9])):
        here = lax.axis_index(axis)
        for step, in_ref in enumerate(inputs):
            out_ref[lax.rem(here - step + 4, 4)] = in_ref[...]


def fetch_kernel(wq_hbm, wk_hbm, wv_hbm, wq_ref, wk_ref, wv_ref, sems):
    copies = [
        pltpu.make_async_copy(wq_hbm, wq_ref, sems.at[0]),
        pltpu.make_async_copy(wk_hbm, wk_ref, sems.at[1]),
        pltpu.make_async_copy(wv_hbm, wv_ref, sems.at[2]),
    ]
    for copy in copies:
        copy.start()
    for copy in copies:
        copy.wait()


def attention_kernel(*refs):
    own_refs, peer_refs = refs[0:4], refs[4:8]
    d_ref, back_refs, (all_ref, dk_ref, dv_ref) = refs[8], refs[9:13], refs[13:]
    y, zl, core = (lax.axis_index(a) for a in ("y", "zl", "core"))
    for step in range(4):
        source = lax.rem(y - step + 4, 4)
        for line in range(4):
            all_ref[source, line, core] = own_refs[step][line]
            all_ref[source, line, 1 - core] = peer_refs[step][line]
    dk_ref[...] = jnp.zeros_like(dk_ref)
    dv_ref[...] = jnp.zeros_like(dv_ref)

    def put(place, part, value):
        value = value.reshape(4, 2, 32, 128)
        for c in range(2):
            d_ref[place, c, :, :, part * 128 : (part + 1) * 128] = value[:, c]

    def rows_of(place):
        return all_ref[place].reshape(256, 512)

    for i in range(4):
        query, grad = rows_of(i)[:, 0:128], rows_of(i)[:, 384:512]
        width = (i + 1) * 256
        keys = jnp.concatenate([rows_of(j)[:, 128:256] for j in range(i + 1)], axis=0)
        values = jnp.concatenate([rows_of(j)[:, 256:384] for j in range(i + 1)], axis=0)
        scores = lax.dot_general(query, keys, NT, preferred_element_type=F32) * SCALE
        q_pos = i * 256 + lax.broadcasted_iota(jnp.int32, (256, width), 0)
        k_pos = lax.broadcasted_iota(jnp.int32, (256, width), 1)
        scores = jnp.where(k_pos <= q_pos, scores, NEG)
        expd = jnp.exp(scores - jnp.max(scores, axis=1, keepdims=True))
        probs = expd * (1.0 / jnp.sum(expd, axis=1, keepdims=True))
        d_prob = lax.dot_general(grad, values, NT, preferred_element_type=F32)
        delta = jnp.sum(probs * d_prob, axis=1, keepdims=True)
        d_score = (probs * (d_prob - delta)).astype(BF16)
        low = probs.astype(BF16)
        put(i, 0, (jnp.dot(d_score, keys, preferred_element_type=F32) * SCALE).astype(BF16))
        dk_ref[0:width, :] += lax.dot_general(d_score, query, TN, preferred_element_type=F32)
        dv_ref[0:width, :] += lax.dot_general(low, grad, TN, preferred_element_type=F32)
    for i in range(4):
        put(i, 1, (dk_ref[i * 256 : (i + 1) * 256, :] * SCALE).astype(BF16))
        put(i, 2, dv_ref[i * 256 : (i + 1) * 256, :].astype(BF16))
    for step in range(4):
        back_refs[step][...] = d_ref[y, core, lax.rem(zl + step, 4)]


def weight_grad_kernel(
    chunk0_ref, chunk1_ref, chunk2_ref, chunk3_ref, d_ref, late0_ref, late1_ref, late2_ref,
    keep_ref, send_ref, made_ref,
):
    zl, core = lax.axis_index("zl"), lax.axis_index("core")
    chunks = (chunk0_ref, chunk1_ref, chunk2_ref, chunk3_ref)
    rows = jnp.concatenate([ref[...].reshape(128, 512) for ref in chunks], axis=0)
    terms = jnp.concatenate(
        [
            d_ref[place, core, lax.rem(zl - step + 4, 4)]
            for step in range(4)
            for place in range(4)
        ],
        axis=0,
    )
    made_ref[...] = lax.dot_general(rows, terms, TN, preferred_element_type=F32).reshape(
        16, 2, 16, 384
    )
    keep_ref[...] = made_ref[:, core]
    send_ref[...] = made_ref[:, 1 - core].astype(BF16)


def join_kernel(keep_ref, got_ref, late_ref, out_ref):
    out_ref[...] = (keep_ref[...] + got_ref[...].astype(F32)).astype(BF16)


def other_half_kernel(
    back0_ref, back1_ref, back2_ref, back3_ref, wq_ref, wk_ref, wv_ref, rows_ref, send_ref
):
    zl = lax.axis_index("zl")
    for step, back_ref in enumerate((back0_ref, back1_ref, back2_ref, back3_ref)):
        rows_ref[lax.rem(zl - step + 4, 4)] = back_ref[...]
    other = 1 - lax.axis_index("zh")
    send_ref[...] = back_project(rows_ref, (wq_ref, wk_ref, wv_ref), other).astype(BF16)


def own_half_kernel(rows_ref, wq_ref, wk_ref, wv_ref, keep_ref):
    keep_ref[...] = back_project(rows_ref, (wq_ref, wk_ref, wv_ref), lax.axis_index("zh"))


def back_project(rows_ref, w_refs, half):
    total = jnp.zeros((32, 1024), F32)
    features = pl.ds(pl.multiple_of(half * 1024, 1024), 1024)
    for part, w_ref in enumerate(w_refs):
        rows = jnp.concatenate(
            [rows_ref[head, :, part * 128 : (part + 1) * 128] for head in range(4)], axis=1
        )
        total = total + lax.dot_general(rows, w_ref[features, :], NT, preferred_element_type=F32)
    return total


def spread_kernel(ids_ref, keep_ref, got_ref, out_ref):
    for block in range(2):
        onehot = slots_of(ids_ref, block)
        rows = slice(block * SLOTS, (block + 1) * SLOTS)
        total = keep_ref[rows, :] + got_ref[rows, :].astype(F32)
        share = (total / jnp.sum(onehot, axis=1, keepdims=True)).astype(BF16)
        out_ref[block * 128 : (block + 1) * 128, :] = lax.dot_general(
            onehot.astype(BF16), share, TN, preferred_element_type=F32
        ).astype(BF16)


def sum_kernel(parts_ref, out0_ref, out1_ref, out2_ref, out3_ref, total_ref):
    zl = lax.axis_index("zl")
    for place in range(4):
        total = parts_ref[0, place].astype(F32)
        for dp in range(1, 4):
            total = total + parts_ref[dp, place].astype(F32)
        total_ref[place] = total
    for step, out_ref in enumerate((out0_ref, out1_ref, out2_ref, out3_ref)):
        out_ref[...] = total_ref[lax.rem(zl + step, 4)]


def place_kernel(in0_ref, in1_ref, in2_ref, in3_ref, q_ref, k_ref, v_ref, total_ref):
    zl = lax.axis_index("zl")
    for step, in_ref in enumerate((in0_ref, in1_ref, in2_ref, in3_ref)):
        total_ref[lax.rem(zl - step + 4, 4)] = in_ref[...]
    for head in range(4):
        for part, out_ref in enumerate((q_ref, k_ref, v_ref)):
            lanes = slice(part * 128, (part + 1) * 128)
            out_ref[:, head * 128 : (head + 1) * 128] = total_ref[head, :, lanes]


def call(kernel, outs, ins, mib, flops, moved, scratch=()):
    spaces = {
        "v": VMEM,
        "h": pl.BlockSpec(memory_space=pltpu.HBM),
    }
    return pl.pallas_call(
        kernel,
        out_shape=tuple(jax.ShapeDtypeStruct(shape, dtype) for shape, dtype in outs),
        in_specs=[spaces[place] for place in ins],
        out_specs=tuple(VMEM for _ in outs),
        scratch_shapes=list(scratch),
        compiler_params=pltpu.CompilerParams(vmem_limit_bytes=mib << 20),
        cost_estimate=pl.CostEstimate(flops=flops, bytes_accessed=moved, transcendentals=0),
    )


def swap(x, axis):
    return lax.ppermute(x, axis, [(0, 1), (1, 0)])


def exchange(x, axes):
    return lax.all_to_all(x, axes, 0, 0, tiled=True)


def turn(x, axis, step):
    return lax.ppermute(x, axis, [(i, (i + step) % 4) for i in range(4)])


def body(byte_states, segment_ids, w_query, w_key, w_value, d_out):
    ids = segment_ids[0]
    weights = (w_query, w_key, w_value)

    with jax.named_scope("pool"):
        (pooled,) = call(
            pool_kernel, [((32, 1024), BF16)], "hh", 62, 10**7, 2 << 20,
            scratch=[
                pltpu.VMEM((2, 128), jnp.int32),
                pltpu.VMEM((256, 1024), BF16),
                pltpu.SemaphoreType.DMA((2,)),
            ],
        )(ids, byte_states[0])
    with jax.named_scope("share_features"):
        pooled_got = swap(pooled, "zh")
    with jax.named_scope("fetch_weights"):
        *weights, _ = lax.optimization_barrier((*weights, pooled))
        weights = call(
            fetch_kernel, [((2048, 512), BF16)] * 3, "hhh", 4, 10**6, 12 << 20,
            scratch=[pltpu.SemaphoreType.DMA((3,))],
        )(*weights)

    with jax.named_scope("project"):
        made = call(
            project_kernel,
            [((32, 512), BF16)] * 8,
            "v" * 6, 10, 2 * 10**8, 8 << 20,
            scratch=[
                pltpu.VMEM((2, 32, 1024), BF16),
                pltpu.VMEM((4, 32, 512), BF16),
                pltpu.VMEM((4, 32, 512), BF16),
            ],
        )(pooled, pooled_got, d_out[0], *weights)
        heads, parts = made[:4], made[4:]

    with jax.named_scope("share_heads"):
        packed, chunk = call(
            stack_kernel, [((4, 32, 512), BF16)] * 2, "v" * 8, 4, 10**5, 1 << 19
        )(
            heads[0], *(turn(heads[step], "zl", step) for step in range(1, 4)),
            parts[0], *(turn(parts[step], "y", step) for step in range(1, 4)),
        )
        own = [packed] + [turn(packed, "y", step) for step in range(1, 4)]
        peer = [swap(x, "core") for x in own]
    with jax.named_scope("share_chunk"):
        chunks = [chunk] + [turn(chunk, "zl", step) for step in range(1, 4)]

    with jax.named_scope("attention"):
        d_rows, *back = call(
            attention_kernel,
            [((4, 2, 4, 32, 384), BF16)] + [((32, 384), BF16)] * 4,
            "v" * 8, 16, 2 * 10**9, 4 << 20,
            scratch=[
                pltpu.VMEM((4, 4, 2, 32, 512), BF16),
                pltpu.VMEM((1024, 128), F32),
                pltpu.VMEM((1024, 128), F32),
            ],
        )(*own, *peer)

    with jax.named_scope("return_rows"):
        back = [back[0]] + [turn(back[step], "zl", step) for step in range(1, 4)]
    with jax.named_scope("back_project"):
        rows, send = call(
            other_half_kernel, [((4, 32, 384), BF16), ((32, 1024), BF16)],
            "v" * 7, 8, 4 * 10**8, 7 << 20,
        )(*back, *weights)
        got = swap(send, "zh")
        (keep,) = call(
            own_half_kernel, [((32, 1024), F32)], "v" * 4, 8, 4 * 10**8, 7 << 20
        )(rows, *weights)

    with jax.named_scope("weight_grads"):
        grad_keep, grad_send = call(
            weight_grad_kernel, [((16, 16, 384), F32), ((16, 16, 384), BF16)], "v" * 5 + "hhh", 10,
            4 * 10**8, 2 << 20, scratch=[pltpu.VMEM((16, 2, 16, 384), F32)],
        )(*chunks, d_rows, *back[1:])
        grad_got = swap(grad_send, "core")
    with jax.named_scope("sum_grads"):
        (partial,) = call(
            join_kernel, [((16, 16, 384), BF16)], "vvh", 4, 10**6, 1 << 20
        )(grad_keep, grad_got, keep)
        parts = exchange(partial.reshape(4, 4, 16, 384), "dp")
        scratch = [pltpu.VMEM((4, 16, 384), F32)]
        sums = call(
            sum_kernel, [((16, 384), F32)] * 4, "v", 4, 10**5, 1 << 20, scratch=scratch
        )(parts)
        sums = [sums[0]] + [turn(sums[step], "zl", step) for step in range(1, 4)]
        grads = call(
            place_kernel, [((16, 512), F32)] * 3, "vvvv", 4, 10**5, 1 << 20, scratch=scratch
        )(*sums)

    with jax.named_scope("spread"):
        (d_bytes,) = call(
            spread_kernel, [((256, 1024), BF16)], "vvv", 4, 10**7, 1 << 20
        )(ids, keep, got)
    return (d_bytes[None], *grads)


def solution(mesh):
    fine = Mesh(
        np.asarray(mesh.devices).reshape(4, 4, 4, 2, 2), ("dp", "y", "zl", "core", "zh")
    )
    seq = ("y", "zl", "core")
    rows = P(("dp", *seq), "zh")
    return jax.shard_map(
        body,
        mesh=fine,
        in_specs=(
            P("dp", seq, "zh"),
            P("dp", seq, None),
            P(None, "zh"),
            P(None, "zh"),
            P(None, "zh"),
            P("dp", seq, "zh"),
        ),
        out_specs=(P("dp", seq, "zh"), rows, rows, rows),
        check_vma=False,
    )
```
